32 devices in a mesh: grp: 2 (over x), feat: 8 (over z, y), tok: 2 (over core).
Axes of the slice: x: 2, y: 2, z: 4, core: 2. Of those that a mesh axis runs over, the one named last changes fastest.
Arguments:
- states: bfloat16 [4096, 8192], P(('grp', 'tok'), 'feat'), parts along dimension 0, may hold values from -6 to 6
Outputs:
- covariance: float32 [16384, 8192], P(('grp', 'tok'), 'feat'), parts along dimension 0
The draws below stay inside these ranges and needn't reach their ends.
There are 2 independent parts, one for each index of `grp`. The reference program is written for one: setup_inputs(seed, part) draws one part's arguments, and reference() takes and returns one part's arrays. A program takes and returns all parts, laid end to end along the dimension named above; each array names one. Nothing has to cross between parts.
All inputs are finite; a program needn't handle non-finite values.
Results may differ from the reference program's by a relative error of at most 0.0003.
Values may be sent and summed in bfloat16 or wider, within the bound.
A program may use at most 192 MiB of HBM per device.

```python
import jax
import jax.numpy as jnp
from jax import lax

D = 8192
TOKENS = 2048


def steps_of(own_key, shape, split, low, largest):
    factor_of, own = 1.0, jax.random.fold_in(own_key, 6)
    for position, blocks in split:
        draws = jnp.exp(jax.random.uniform(jax.random.fold_in(own, position), (blocks,), jnp.float32, low / len(split), largest / len(split)))
        factor_of = factor_of * jnp.repeat(draws, shape[position] // blocks).reshape([-1 if axis == position else 1 for axis in range(len(shape))])
    return factor_of


def gaussian(key, extent, scale, reach, cuts=(), kind=jnp.bfloat16):
    loudness = steps_of(key, extent, cuts, -0.22, 0.18) if cuts else 1.0
    values = jax.random.normal(key, extent, jnp.float32) * scale * loudness
    return jnp.minimum(jnp.maximum(values, -reach), reach).astype(kind)


def setup_inputs(seed: int = 0, part: int = 0) -> dict:
    key_of = jax.random.split(jax.random.key(seed), 2)
    own_keys = jax.random.split(jax.random.fold_in(key_of[1], part), 2)
    return {
        "states": gaussian(own_keys[0], (TOKENS, D), 1.0, 6.0, ((0, 2), (1, 8))),
    }


def reference(states):
    product = lax.dot_general(states, states, (((0,), (0,)), ((), ())), preferred_element_type=jnp.float32)
    return product / jnp.float32(TOKENS)
```

```python
import functools

import jax
import jax.numpy as jnp
from jax import lax
from jax.experimental import pallas as pl
from jax.experimental.pallas import tpu as pltpu
from jax.sharding import PartitionSpec as P

MESH = pl.DeviceIdType.MESH


def feature_of(place, n, snake):
    if not snake:
        return place
    back = place // (n // 2)
    return (1 - back) * 2 * place + back * (2 * (n - 1 - place) + 1)


def place_of(feature, n, snake):
    if not snake:
        return feature
    odd = feature % 2
    return (1 - odd) * (feature // 2) + odd * (n - 1 - feature // 2)


def kernel(
    n, pieces, snake, tokens, x_ref, out_ref, held, other, stage,
    ring_send, ring_recv, pair_send, pair_recv, load_sem, store_sem,
):
    width = held.shape[-1]
    block = width * pieces
    half = n // 2
    me = lax.axis_index("feat")
    tok = lax.axis_index("tok")
    place = place_of(me, n, snake)

    def at_distance(steps):
        return feature_of((place + steps + n) % n, n, snake)

    def origin(arrival, piece):
        return at_distance((2 * (piece % 2) - 1) * arrival)

    def partner(piece):
        return at_distance(1 - 2 * (piece % 2))

    def ring(arrival, piece, feature, src=None):
        return pltpu.make_async_remote_copy(
            src_ref=held.at[feature, piece] if src is None else src,
            dst_ref=held.at[feature, piece],
            send_sem=ring_send.at[arrival - 1, piece],
            recv_sem=ring_recv.at[arrival - 1, piece],
            device_id={"feat": partner(piece)},
            device_id_type=MESH,
        )

    def pair(slot, piece, src):
        return pltpu.make_async_remote_copy(
            src_ref=src,
            dst_ref=other.at[slot, piece],
            send_sem=pair_send.at[slot, piece],
            recv_sem=pair_recv.at[slot, piece],
            device_id={"tok": 1 - tok},
            device_id_type=MESH,
        )

    def load(piece):
        return pltpu.make_async_copy(
            x_ref.at[:, pl.ds(piece * width, width)], held.at[me, piece], load_sem.at[piece]
        )

    def store(slot, piece):
        rows = pl.ds(pl.multiple_of(slot * block + piece * width, width), width)
        return pltpu.make_async_copy(
            stage.at[slot, piece], out_ref.at[rows, :], store_sem.at[slot, piece]
        )

    barrier = pltpu.get_barrier_semaphore()
    for where in ({"feat": at_distance(1)}, {"feat": at_distance(-1)}, {"tok": 1 - tok}):
        pl.semaphore_signal(barrier, inc=1, device_id=where, device_id_type=MESH)
    pl.semaphore_wait(barrier, 3)

    for piece in range(pieces):
        part = x_ref.at[:, pl.ds(piece * width, width)]
        ring(1, piece, me, part).start()
        load(piece).start()
    for piece in range(pieces):
        pair(half, piece, x_ref.at[:, pl.ds(piece * width, width)]).start()
    for piece in range(pieces):
        load(piece).wait()
    for piece in range(pieces):
        pair(half, piece, held.at[me, piece]).wait_recv()

    def multiply(feature, piece, from_other):
        slot = feature % half
        first = held[feature, piece].T
        second = other[from_other, piece].T
        for column in range(pieces):
            total = jnp.dot(first, held[me, column], preferred_element_type=jnp.float32)
            total += jnp.dot(second, other[half, column], preferred_element_type=jnp.float32)
            stage[slot, piece, :, column * width:(column + 1) * width] = total / jnp.float32(tokens)
        store(slot, piece).start()

    def compute(arrival, piece):
        feature = origin(arrival, piece)
        slot = feature % half

        @pl.when(feature // half == tok)
        def _():
            @pl.when(arrival > 0)
            def _():
                pair(slot, piece, held.at[feature, piece]).wait_recv()

            own = 1 - (arrival + n - 1) // n
            multiply(feature, piece, own * half + (1 - own) * slot)

    @pl.loop(1, n)
    def _(arrival):
        @pl.loop(0, pieces)
        def _(piece):
            feature = origin(arrival, piece)
            ring(arrival, piece, feature).wait_recv()

            @pl.when(arrival < n - 1)
            def _():
                ring(arrival + 1, piece, feature).start()

            @pl.when(feature // half != tok)
            def _():
                pair(feature % half, piece, held.at[feature, piece]).start()

            compute(arrival - 1, piece)

    @pl.loop(0, pieces)
    def _(piece):
        compute(n - 1, piece)

    @pl.loop(0, pieces)
    def _(piece):
        @pl.loop(1, n)
        def _(arrival):
            feature = origin(arrival, piece)
            ring(arrival, piece, feature).wait_send()

            @pl.when(feature // half != tok)
            def _():
                pair(feature % half, piece, held.at[feature, piece]).wait_send()

        pair(half, piece, held.at[me, piece]).wait_send()

        @pl.loop(0, half)
        def _(slot):
            store(slot, piece).wait()


def solution(mesh):
    n = mesh.shape["feat"]
    snake = mesh.shape["grp"] == 2

    def shards(states):
        rows, block = states.shape
        tokens = rows * mesh.shape["tok"]
        pieces = max(2, min(4, block // 128))
        width = block // pieces
        half = n // 2
        return pl.pallas_call(
            functools.partial(kernel, n, pieces, snake, tokens),
            out_shape=jax.ShapeDtypeStruct((half * block, block), jnp.float32),
            in_specs=[pl.BlockSpec(memory_space=pl.ANY)],
            out_specs=pl.BlockSpec(memory_space=pl.ANY),
            scratch_shapes=[
                pltpu.VMEM((n, pieces, rows, width), states.dtype),
                pltpu.VMEM((half + 1, pieces, rows, width), states.dtype),
                pltpu.VMEM((half, pieces, width, block), jnp.float32),
                pltpu.SemaphoreType.DMA((n - 1, pieces)),
                pltpu.SemaphoreType.DMA((n - 1, pieces)),
                pltpu.SemaphoreType.DMA((half + 1, pieces)),
                pltpu.SemaphoreType.DMA((half + 1, pieces)),
                pltpu.SemaphoreType.DMA((pieces,)),
                pltpu.SemaphoreType.DMA((half, pieces)),
            ],
            compiler_params=pltpu.CompilerParams(
                collective_id=0, has_side_effects=True, vmem_limit_bytes=56 * 2**20
            ),
            cost_estimate=pl.CostEstimate(
                flops=2 * half * block * block * tokens,
                bytes_accessed=half * block * block * 4 + rows * block * 2,
                transcendentals=0,
            ),
        )(states)

    placed = P(("grp", "tok"), "feat")
    return jax.shard_map(
        shards, mesh=mesh, in_specs=(placed,), out_specs=placed, check_vma=False
    )
```

```python
import functools

import jax
import jax.numpy as jnp
from jax import lax
from jax.experimental import pallas as pl
from jax.experimental.pallas import tpu as pltpu
from jax.sharding import PartitionSpec as P

MESH = pl.DeviceIdType.MESH


def feature_of(place, n, snake):
    if not snake:
        return place
    back = place // (n // 2)
    return (1 - back) * 2 * place + back * (2 * (n - 1 - place) + 1)


def place_of(feature, n, snake):
    if not snake:
        return feature
    odd = feature % 2
    return (1 - odd) * (feature // 2) + odd * (n - 1 - feature // 2)


def kernel(
    n, pieces, snake, tokens, x_ref, stage, held, other,
    ring_send, ring_recv, pair_send, pair_recv, load_sem,
):
    width = held.shape[-1]
    block = width * pieces
    half = n // 2
    me = lax.axis_index("feat")
    tok = lax.axis_index("tok")
    place = place_of(me, n, snake)

    def at_distance(steps):
        return feature_of((place + steps + n) % n, n, snake)

    def origin(arrival, piece):
        return at_distance((2 * (piece % 2) - 1) * arrival)

    def partner(piece):
        return at_distance(1 - 2 * (piece % 2))

    def ring(arrival, piece, feature, src=None):
        return pltpu.make_async_remote_copy(
            src_ref=held.at[feature, piece] if src is None else src,
            dst_ref=held.at[feature, piece],
            send_sem=ring_send.at[arrival - 1, piece],
            recv_sem=ring_recv.at[arrival - 1, piece],
            device_id={"feat": partner(piece)},
            device_id_type=MESH,
        )

    def pair(slot, piece, src):
        return pltpu.make_async_remote_copy(
            src_ref=src,
            dst_ref=other.at[slot, piece],
            send_sem=pair_send.at[slot, piece],
            recv_sem=pair_recv.at[slot, piece],
            device_id={"tok": 1 - tok},
            device_id_type=MESH,
        )

    def load(piece):
        return pltpu.make_async_copy(
            x_ref.at[:, pl.ds(piece * width, width)], held.at[me, piece], load_sem.at[piece]
        )

    barrier = pltpu.get_barrier_semaphore()
    for where in ({"feat": at_distance(1)}, {"feat": at_distance(-1)}, {"tok": 1 - tok}):
        pl.semaphore_signal(barrier, inc=1, device_id=where, device_id_type=MESH)
    pl.semaphore_wait(barrier, 3)

    for piece in range(pieces):
        part = x_ref.at[:, pl.ds(piece * width, width)]
        ring(1, piece, me, part).start()
        load(piece).start()
    for piece in range(pieces):
        pair(half, piece, x_ref.at[:, pl.ds(piece * width, width)]).start()
    for piece in range(pieces):
        load(piece).wait()
    for piece in range(pieces):
        pair(half, piece, held.at[me, piece]).wait_recv()

    def multiply(feature, piece, from_other):
        slot = feature % half
        first = held[feature, piece].T
        second = other[from_other, piece].T
        for column in range(pieces):
            total = jnp.dot(first, held[me, column], preferred_element_type=jnp.float32)
            total += jnp.dot(second, other[half, column], preferred_element_type=jnp.float32)
            stage[slot, piece, :, column * width:(column + 1) * width] = total / jnp.float32(tokens)

    def compute(arrival, piece):
        feature = origin(arrival, piece)
        slot = feature % half

        @pl.when(feature // half == tok)
        def _():
            @pl.when(arrival > 0)
            def _():
                pair(slot, piece, held.at[feature, piece]).wait_recv()

            own = 1 - (arrival + n - 1) // n
            multiply(feature, piece, own * half + (1 - own) * slot)

    @pl.loop(1, n)
    def _(arrival):
        @pl.loop(0, pieces)
        def _(piece):
            feature = origin(arrival, piece)
            ring(arrival, piece, feature).wait_recv()

            @pl.when(arrival < n - 1)
            def _():
                ring(arrival + 1, piece, feature).start()

            @pl.when(feature // half != tok)
            def _():
                pair(feature % half, piece, held.at[feature, piece]).start()

            compute(arrival - 1, piece)

    @pl.loop(0, pieces)
    def _(piece):
        compute(n - 1, piece)

    @pl.loop(0, pieces)
    def _(piece):
        @pl.loop(1, n)
        def _(arrival):
            feature = origin(arrival, piece)
            ring(arrival, piece, feature).wait_send()

            @pl.when(feature // half != tok)
            def _():
                pair(feature % half, piece, held.at[feature, piece]).wait_send()

        pair(half, piece, held.at[me, piece]).wait_send()


def write_out(pieces, product_ref, out_ref, sem):
    half, _, width, _ = product_ref.shape
    copies = [
        pltpu.make_async_copy(
            product_ref.at[slot, piece],
            out_ref.at[pl.ds((slot * pieces + piece) * width, width), :],
            sem.at[slot, piece],
        )
        for slot in range(half)
        for piece in range(pieces)
    ]
    for copy in copies:
        copy.start()
    for copy in copies:
        copy.wait()


def solution(mesh):
    n = mesh.shape["feat"]
    snake = mesh.shape["grp"] == 2

    def shards(states):
        rows, block = states.shape
        tokens = rows * mesh.shape["tok"]
        pieces = max(2, min(4, block // 128))
        width = block // pieces
        half = n // 2
        product = pl.pallas_call(
            functools.partial(kernel, n, pieces, snake, tokens),
            out_shape=pltpu.VMEM((half, pieces, width, block), jnp.float32),
            in_specs=[pl.BlockSpec(memory_space=pl.ANY)],
            out_specs=pl.BlockSpec(memory_space=pltpu.VMEM),
            scratch_shapes=[
                pltpu.VMEM((n, pieces, rows, width), states.dtype),
                pltpu.VMEM((half + 1, pieces, rows, width), states.dtype),
                pltpu.SemaphoreType.DMA((n - 1, pieces)),
                pltpu.SemaphoreType.DMA((n - 1, pieces)),
                pltpu.SemaphoreType.DMA((half + 1, pieces)),
                pltpu.SemaphoreType.DMA((half + 1, pieces)),
                pltpu.SemaphoreType.DMA((pieces,)),
            ],
            compiler_params=pltpu.CompilerParams(
                collective_id=0, has_side_effects=True, vmem_limit_bytes=36 * 2**20
            ),
            cost_estimate=pl.CostEstimate(
                flops=2 * half * block * block * tokens,
                bytes_accessed=half * block * block * 4 + rows * block * 2,
                transcendentals=0,
            ),
        )(states)
        return pl.pallas_call(
            functools.partial(write_out, pieces),
            out_shape=jax.ShapeDtypeStruct((half * block, block), jnp.float32),
            in_specs=[pl.BlockSpec(memory_space=pltpu.VMEM)],
            out_specs=pl.BlockSpec(memory_space=pl.ANY),
            scratch_shapes=[pltpu.SemaphoreType.DMA((half, pieces))],
            compiler_params=pltpu.CompilerParams(vmem_limit_bytes=2**20),
        )(pltpu.with_memory_space_constraint(product, pltpu.VMEM))

    placed = P(("grp", "tok"), "feat")
    return jax.shard_map(
        shards, mesh=mesh, in_specs=(placed,), out_specs=placed, check_vma=False
    )
```

```python
import functools

import jax
import jax.numpy as jnp
from jax import lax
from jax.experimental import pallas as pl
from jax.experimental.pallas import tpu as pltpu
from jax.sharding import PartitionSpec as P

MESH = pl.DeviceIdType.MESH


def feature_of(place, n, snake):
    if not snake:
        return place
    back = place // (n // 2)
    return (1 - back) * 2 * place + back * (2 * (n - 1 - place) + 1)


def place_of(feature, n, snake):
    if not snake:
        return feature
    odd = feature % 2
    return (1 - odd) * (feature // 2) + odd * (n - 1 - feature // 2)


def position(n, snake):
    tok = lax.axis_index("tok")
    place = place_of(lax.axis_index("feat"), n, snake)

    def at_distance(steps):
        return feature_of((place + steps + n) % n, n, snake)

    def origin(arrival, piece):
        return at_distance((2 * (piece % 2) - 1) * arrival)

    return tok, at_distance, origin


def multiply(held, other, feature, piece, from_other, tokens, target):
    pieces, _, width = held.shape[1:]
    own = other.shape[0] - 1
    me = lax.axis_index("feat")
    first = held[feature, piece].T
    second = other[from_other, piece].T
    for column in range(pieces):
        total = jnp.dot(first, held[me, column], preferred_element_type=jnp.float32)
        total += jnp.dot(second, other[own, column], preferred_element_type=jnp.float32)
        target[:, column * width:(column + 1) * width] = total / jnp.float32(tokens)


def gather_and_multiply(
    n, snake, tokens, x_ref, product, held, other,
    ring_send, ring_recv, pair_send, pair_recv, load_sem,
):
    _, pieces, _, width = held.shape
    half = n // 2
    last = n - 1
    me = lax.axis_index("feat")
    tok, at_distance, origin = position(n, snake)

    def partner(piece):
        return at_distance(1 - 2 * (piece % 2))

    def ring(arrival, piece, feature, src=None):
        return pltpu.make_async_remote_copy(
            src_ref=held.at[feature, piece] if src is None else src,
            dst_ref=held.at[feature, piece],
            send_sem=ring_send.at[arrival - 1, piece],
            recv_sem=ring_recv.at[arrival - 1, piece],
            device_id={"feat": partner(piece)},
            device_id_type=MESH,
        )

    def across(piece, feature):
        return pltpu.make_async_remote_copy(
            src_ref=held.at[feature, piece],
            dst_ref=other.at[feature % half, piece],
            send_sem=ring_send.at[last - 1, piece],
            recv_sem=pair_recv.at[feature % half, piece],
            device_id={"feat": partner(piece), "tok": 1 - tok},
            device_id_type=MESH,
        )

    def pair(slot, piece, src):
        return pltpu.make_async_remote_copy(
            src_ref=src,
            dst_ref=other.at[slot, piece],
            send_sem=pair_send.at[slot, piece],
            recv_sem=pair_recv.at[slot, piece],
            device_id={"tok": 1 - tok},
            device_id_type=MESH,
        )

    def load(piece):
        return pltpu.make_async_copy(
            x_ref.at[:, pl.ds(piece * width, width)], held.at[me, piece], load_sem.at[piece]
        )

    barrier = pltpu.get_barrier_semaphore()
    for where in (
        {"feat": at_distance(1)},
        {"feat": at_distance(-1)},
        {"tok": 1 - tok},
        {"feat": at_distance(1), "tok": 1 - tok},
        {"feat": at_distance(-1), "tok": 1 - tok},
    ):
        pl.semaphore_signal(barrier, inc=1, device_id=where, device_id_type=MESH)
    pl.semaphore_wait(barrier, 5)

    for piece in range(pieces):
        part = x_ref.at[:, pl.ds(piece * width, width)]
        ring(1, piece, me, part).start()
        load(piece).start()
    for piece in range(pieces):
        pair(half, piece, x_ref.at[:, pl.ds(piece * width, width)]).start()
    for piece in range(pieces):
        load(piece).wait()
    for piece in range(pieces):
        pair(half, piece, held.at[me, piece]).wait_recv()

    def compute(arrival, piece):
        feature = origin(arrival, piece)
        slot = feature % half

        @pl.when(feature // half == tok)
        def _():
            @pl.when(arrival > 0)
            def _():
                pair(slot, piece, held.at[feature, piece]).wait_recv()

            own = 1 - (arrival + n - 1) // n
            from_other = own * half + (1 - own) * slot
            multiply(held, other, feature, piece, from_other, tokens, product.at[slot, piece])

    @pl.loop(1, last)
    def _(arrival):
        @pl.loop(0, pieces)
        def _(piece):
            feature = origin(arrival, piece)
            mine = feature // half == tok
            ring(arrival, piece, feature).wait_recv()

            @pl.when((arrival < last - 1) | mine)
            def _():
                ring(arrival + 1, piece, feature).start()

            @pl.when((arrival == last - 1) & (feature // half != tok))
            def _():
                across(piece, feature).start()

            @pl.when(feature // half != tok)
            def _():
                pair(feature % half, piece, held.at[feature, piece]).start()

            compute(arrival - 1, piece)

    @pl.loop(0, pieces)
    def _(piece):
        compute(last - 1, piece)

    @pl.loop(0, pieces)
    def _(piece):
        @pl.loop(1, last)
        def _(arrival):
            feature = origin(arrival, piece)
            ring(arrival, piece, feature).wait_send()

            @pl.when(feature // half != tok)
            def _():
                pair(feature % half, piece, held.at[feature, piece]).wait_send()

        pair(half, piece, held.at[me, piece]).wait_send()

    @pl.loop(0, pieces)
    def _(piece):
        feature = origin(last, piece)
        ring(last, piece, feature).wait_send()

        @pl.when(feature // half == tok)
        def _():
            ring(last, piece, feature).wait_recv()
            pair(feature % half, piece, held.at[feature, piece]).wait_recv()


def finish(n, snake, tokens, product, held, other, out_ref, late, sem):
    half, pieces, width, _ = product.shape
    tok, _, origin = position(n, snake)

    def store(slot, piece, src):
        rows = pl.ds(pl.multiple_of((slot * pieces + piece) * width, width), width)
        return pltpu.make_async_copy(src, out_ref.at[rows, :], sem.at[slot, piece])

    @pl.loop(0, half)
    def _(slot):
        @pl.loop(0, pieces)
        def _(piece):
            @pl.when(origin(n - 1, piece) != tok * half + slot)
            def _():
                store(slot, piece, product.at[slot, piece]).start()

    @pl.loop(0, pieces)
    def _(piece):
        feature = origin(n - 1, piece)
        slot = feature % half

        @pl.when(feature // half == tok)
        def _():
            multiply(held, other, feature, piece, slot, tokens, late.at[piece])
            store(slot, piece, late.at[piece]).start()

    @pl.loop(0, half)
    def _(slot):
        @pl.loop(0, pieces)
        def _(piece):
            store(slot, piece, product.at[slot, piece]).wait()


def solution(mesh):
    n = mesh.shape["feat"]
    snake = mesh.shape["grp"] == 2

    def shards(states):
        rows, block = states.shape
        tokens = rows * mesh.shape["tok"]
        pieces = max(2, min(4, block // 128))
        width = block // pieces
        half = n // 2
        gathered = pl.pallas_call(
            functools.partial(gather_and_multiply, n, snake, tokens),
            out_shape=(
                pltpu.VMEM((half, pieces, width, block), jnp.float32),
                pltpu.VMEM((n, pieces, rows, width), states.dtype),
                pltpu.VMEM((half + 1, pieces, rows, width), states.dtype),
            ),
            in_specs=[pl.BlockSpec(memory_space=pl.ANY)],
            out_specs=(pl.BlockSpec(memory_space=pltpu.VMEM),) * 3,
            scratch_shapes=[
                pltpu.SemaphoreType.DMA((n - 1, pieces)),
                pltpu.SemaphoreType.DMA((n - 1, pieces)),
                pltpu.SemaphoreType.DMA((half + 1, pieces)),
                pltpu.SemaphoreType.DMA((half + 1, pieces)),
                pltpu.SemaphoreType.DMA((pieces,)),
            ],
            compiler_params=pltpu.CompilerParams(
                collective_id=0, has_side_effects=True, vmem_limit_bytes=8 * 2**20
            ),
            cost_estimate=pl.CostEstimate(
                flops=2 * half * block * block * tokens,
                bytes_accessed=half * block * block * 4 + rows * block * 2,
                transcendentals=0,
            ),
        )(states)
        return pl.pallas_call(
            functools.partial(finish, n, snake, tokens),
            out_shape=jax.ShapeDtypeStruct((half * block, block), jnp.float32),
            in_specs=[pl.BlockSpec(memory_space=pltpu.VMEM)] * 3,
            out_specs=pl.BlockSpec(memory_space=pl.ANY),
            scratch_shapes=[
                pltpu.VMEM((pieces, width, block), jnp.float32),
                pltpu.SemaphoreType.DMA((half, pieces)),
            ],
            compiler_params=pltpu.CompilerParams(vmem_limit_bytes=10 * 2**20),
        )(*(pltpu.with_memory_space_constraint(part, pltpu.VMEM) for part in gathered))

    placed = P(("grp", "tok"), "feat")
    return jax.shard_map(
        shards, mesh=mesh, in_specs=(placed,), out_specs=placed, check_vma=False
    )
```

```python
import functools

import jax
import jax.numpy as jnp
from jax import lax
from jax.experimental import pallas as pl
from jax.experimental.pallas import tpu as pltpu
from jax.sharding import PartitionSpec as P

MESH = pl.DeviceIdType.MESH


def feature_of(place, n, snake):
    if not snake:
        return place
    back = place // (n // 2)
    return (1 - back) * 2 * place + back * (2 * (n - 1 - place) + 1)


def place_of(feature, n, snake):
    if not snake:
        return feature
    odd = feature % 2
    return (1 - odd) * (feature // 2) + odd * (n - 1 - feature // 2)


def position(n, snake):
    tok = lax.axis_index("tok")
    place = place_of(lax.axis_index("feat"), n, snake)

    def at_distance(steps):
        return feature_of((place + steps + n) % n, n, snake)

    def origin(arrival, piece):
        return at_distance((2 * (piece % 2) - 1) * arrival)

    return tok, at_distance, origin


def multiply(held, other, feature, piece, from_other, tokens, target):
    pieces, _, width = held.shape[1:]
    own = other.shape[0] - 1
    me = lax.axis_index("feat")
    first = held[feature, piece].T
    second = other[from_other, piece].T
    for column in range(pieces):
        total = jnp.dot(first, held[me, column], preferred_element_type=jnp.float32)
        total += jnp.dot(second, other[own, column], preferred_element_type=jnp.float32)
        target[:, column * width:(column + 1) * width] = total / jnp.float32(tokens)


def gather_and_multiply(
    n, snake, tokens, x_ref, product, held, other,
    ring_send, ring_recv, pair_send, pair_recv, load_sem,
):
    _, pieces, _, width = held.shape
    half = n // 2
    last = n - 1
    me = lax.axis_index("feat")
    tok, at_distance, origin = position(n, snake)

    def partner(piece):
        return at_distance(1 - 2 * (piece % 2))

    def ring(arrival, piece, feature, src=None):
        return pltpu.make_async_remote_copy(
            src_ref=held.at[feature, piece] if src is None else src,
            dst_ref=held.at[feature, piece],
            send_sem=ring_send.at[arrival - 1, piece],
            recv_sem=ring_recv.at[arrival - 1, piece],
            device_id={"feat": partner(piece)},
            device_id_type=MESH,
        )

    def across(piece, feature):
        return pltpu.make_async_remote_copy(
            src_ref=held.at[feature, piece],
            dst_ref=other.at[feature % half, piece],
            send_sem=ring_send.at[last - 1, piece],
            recv_sem=pair_recv.at[feature % half, piece],
            device_id={"feat": partner(piece), "tok": 1 - tok},
            device_id_type=MESH,
        )

    def pair(slot, piece, src):
        return pltpu.make_async_remote_copy(
            src_ref=src,
            dst_ref=other.at[slot, piece],
            send_sem=pair_send.at[slot, piece],
            recv_sem=pair_recv.at[slot, piece],
            device_id={"tok": 1 - tok},
            device_id_type=MESH,
        )

    def load(piece):
        return pltpu.make_async_copy(
            x_ref.at[:, pl.ds(piece * width, width)], held.at[me, piece], load_sem.at[piece]
        )

    barrier = pltpu.get_barrier_semaphore()
    for where in (
        {"feat": at_distance(1)},
        {"feat": at_distance(-1)},
        {"tok": 1 - tok},
        {"feat": at_distance(1), "tok": 1 - tok},
        {"feat": at_distance(-1), "tok": 1 - tok},
    ):
        pl.semaphore_signal(barrier, inc=1, device_id=where, device_id_type=MESH)
    pl.semaphore_wait(barrier, 5)

    for piece in range(pieces):
        part = x_ref.at[:, pl.ds(piece * width, width)]
        ring(1, piece, me, part).start()
        load(piece).start()
    for piece in range(pieces):
        pair(half, piece, x_ref.at[:, pl.ds(piece * width, width)]).start()
    for piece in range(pieces):
        load(piece).wait()
    for piece in range(pieces):
        pair(half, piece, held.at[me, piece]).wait_recv()

    def compute(arrival, piece):
        feature = origin(arrival, piece)
        slot = feature % half

        @pl.when(feature // half == tok)
        def _():
            @pl.when(arrival > 0)
            def _():
                pair(slot, piece, held.at[feature, piece]).wait_recv()

            own = 1 - (arrival + n - 1) // n
            from_other = own * half + (1 - own) * slot
            multiply(held, other, feature, piece, from_other, tokens, product.at[slot, piece])

    @pl.loop(1, last)
    def _(arrival):
        @pl.loop(0, pieces)
        def _(piece):
            feature = origin(arrival, piece)
            mine = feature // half == tok
            ring(arrival, piece, feature).wait_recv()

            @pl.when((arrival < last - 1) | mine)
            def _():
                ring(arrival + 1, piece, feature).start()

            @pl.when((arrival == last - 1) & (feature // half != tok))
            def _():
                across(piece, feature).start()

            @pl.when(feature // half != tok)
            def _():
                pair(feature % half, piece, held.at[feature, piece]).start()

            compute(arrival - 1, piece)

    @pl.loop(0, pieces)
    def _(piece):
        compute(last - 1, piece)

    @pl.loop(0, pieces)
    def _(piece):
        @pl.loop(1, last)
        def _(arrival):
            feature = origin(arrival, piece)
            ring(arrival, piece, feature).wait_send()

            @pl.when(feature // half != tok)
            def _():
                pair(feature % half, piece, held.at[feature, piece]).wait_send()

        pair(half, piece, held.at[me, piece]).wait_send()

    @pl.loop(0, pieces)
    def _(piece):
        feature = origin(last, piece)
        ring(last, piece, feature).wait_send()

        @pl.when(feature // half == tok)
        def _():
            ring(last, piece, feature).wait_recv()
            pair(feature % half, piece, held.at[feature, piece]).wait_recv()


def finish(n, snake, tokens, product, held, other, out_ref, late, sem):
    half, pieces, width, _ = product.shape
    tok, _, origin = position(n, snake)

    def store(slot, piece, src):
        rows = pl.ds(pl.multiple_of((slot * pieces + piece) * width, width), width)
        return pltpu.make_async_copy(src, out_ref.at[rows, :], sem.at[slot, piece])

    @pl.loop(0, half)
    def _(slot):
        @pl.loop(0, pieces)
        def _(piece):
            @pl.when(origin(n - 1, piece) != tok * half + slot)
            def _():
                store(slot, piece, product.at[slot, piece]).start()

    @pl.loop(0, pieces)
    def _(piece):
        feature = origin(n - 1, piece)
        slot = feature % half

        @pl.when(feature // half == tok)
        def _():
            multiply(held, other, feature, piece, slot, tokens, late.at[piece])
            store(slot, piece, late.at[piece]).start()

    @pl.loop(0, half)
    def _(slot):
        @pl.loop(0, pieces)
        def _(piece):
            store(slot, piece, product.at[slot, piece]).wait()


def solution(mesh):
    n = mesh.shape["feat"]
    snake = mesh.shape["grp"] == 2

    def shards(states):
        rows, block = states.shape
        tokens = rows * mesh.shape["tok"]
        pieces = max(2, min(4, block // 128))
        width = block // pieces
        half = n // 2
        gathered = pl.pallas_call(
            functools.partial(gather_and_multiply, n, snake, tokens),
            out_shape=(
                pltpu.VMEM((half, pieces, width, block), jnp.float32),
                pltpu.VMEM((n, pieces, rows, width), states.dtype),
                pltpu.VMEM((half + 1, pieces, rows, width), states.dtype),
            ),
            in_specs=[pl.BlockSpec(memory_space=pl.ANY)],
            out_specs=(pl.BlockSpec(memory_space=pltpu.VMEM),) * 3,
            scratch_shapes=[
                pltpu.SemaphoreType.DMA((n - 1, pieces)),
                pltpu.SemaphoreType.DMA((n - 1, pieces)),
                pltpu.SemaphoreType.DMA((half + 1, pieces)),
                pltpu.SemaphoreType.DMA((half + 1, pieces)),
                pltpu.SemaphoreType.DMA((pieces,)),
            ],
            compiler_params=pltpu.CompilerParams(
                collective_id=0, has_side_effects=True, vmem_limit_bytes=10 * 2**20
            ),
            cost_estimate=pl.CostEstimate(
                flops=2 * half * block * block * tokens,
                bytes_accessed=half * block * block * 4 + rows * block * 2,
                transcendentals=0,
            ),
        )(states)
        return pl.pallas_call(
            functools.partial(finish, n, snake, tokens),
            out_shape=jax.ShapeDtypeStruct((half * block, block), jnp.float32),
            in_specs=[pl.BlockSpec(memory_space=pltpu.VMEM)] * 3,
            out_specs=pl.BlockSpec(memory_space=pl.ANY),
            scratch_shapes=[
                pltpu.VMEM((pieces, width, block), jnp.float32),
                pltpu.SemaphoreType.DMA((half, pieces)),
            ],
            compiler_params=pltpu.CompilerParams(vmem_limit_bytes=10 * 2**20),
        )(*(pltpu.with_memory_space_constraint(part, pltpu.VMEM) for part in gathered))

    placed = P(("grp", "tok"), "feat")
    return jax.shard_map(
        shards, mesh=mesh, in_specs=(placed,), out_specs=placed, check_vma=False
    )
```

```python
import functools

import jax
import jax.numpy as jnp
from jax import lax
from jax.experimental import pallas as pl
from jax.experimental.pallas import tpu as pltpu
from jax.sharding import PartitionSpec as P

MESH = pl.DeviceIdType.MESH


def feature_of(place, n, snake):
    if not snake:
        return place
    back = place // (n // 2)
    return (1 - back) * 2 * place + back * (2 * (n - 1 - place) + 1)


def place_of(feature, n, snake):
    if not snake:
        return feature
    odd = feature % 2
    return (1 - odd) * (feature // 2) + odd * (n - 1 - feature // 2)


def position(n, snake):
    tok = lax.axis_index("tok")
    place = place_of(lax.axis_index("feat"), n, snake)

    def at_distance(steps):
        return feature_of((place + steps + n) % n, n, snake)

    def origin(arrival, piece):
        return at_distance((2 * (piece % 2) - 1) * arrival)

    return tok, at_distance, origin


def multiply(held, other, feature, piece, from_other, tokens, target):
    pieces, _, width = held.shape[1:]
    own = other.shape[0] - 1
    me = lax.axis_index("feat")
    first = held[feature, piece].T
    second = other[from_other, piece].T
    for column in range(pieces):
        total = jnp.dot(first, held[me, column], preferred_element_type=jnp.float32)
        total += jnp.dot(second, other[own, column], preferred_element_type=jnp.float32)
        target[:, column * width:(column + 1) * width] = total / jnp.float32(tokens)


def gather_and_multiply(
    n, snake, tokens, x_ref, product, held, other,
    ring_send, ring_recv, pair_send, pair_recv, load_sem,
):
    _, pieces, _, width = held.shape
    half = n // 2
    last = n - 1
    me = lax.axis_index("feat")
    tok, at_distance, origin = position(n, snake)

    def partner(piece):
        return at_distance(1 - 2 * (piece % 2))

    def ring(arrival, piece, feature, src=None):
        return pltpu.make_async_remote_copy(
            src_ref=held.at[feature, piece] if src is None else src,
            dst_ref=held.at[feature, piece],
            send_sem=ring_send.at[arrival - 1, piece],
            recv_sem=ring_recv.at[arrival - 1, piece],
            device_id={"feat": partner(piece)},
            device_id_type=MESH,
        )

    def across(piece, feature):
        return pltpu.make_async_remote_copy(
            src_ref=held.at[feature, piece],
            dst_ref=other.at[feature % half, piece],
            send_sem=ring_send.at[last - 1, piece],
            recv_sem=pair_recv.at[feature % half, piece],
            device_id={"feat": partner(piece), "tok": 1 - tok},
            device_id_type=MESH,
        )

    def pair(slot, piece, src):
        return pltpu.make_async_remote_copy(
            src_ref=src,
            dst_ref=other.at[slot, piece],
            send_sem=pair_send.at[slot, piece],
            recv_sem=pair_recv.at[slot, piece],
            device_id={"tok": 1 - tok},
            device_id_type=MESH,
        )

    def load(piece):
        return pltpu.make_async_copy(
            x_ref.at[:, pl.ds(piece * width, width)], held.at[me, piece], load_sem.at[piece]
        )

    barrier = pltpu.get_barrier_semaphore()
    for where in (
        {"feat": at_distance(1)},
        {"feat": at_distance(-1)},
        {"tok": 1 - tok},
        {"feat": at_distance(1), "tok": 1 - tok},
        {"feat": at_distance(-1), "tok": 1 - tok},
    ):
        pl.semaphore_signal(barrier, inc=1, device_id=where, device_id_type=MESH)
    pl.semaphore_wait(barrier, 5)

    for piece in range(pieces):
        part = x_ref.at[:, pl.ds(piece * width, width)]
        ring(1, piece, me, part).start()
        load(piece).start()
    for piece in range(pieces):
        pair(half, piece, x_ref.at[:, pl.ds(piece * width, width)]).start()
    for piece in range(pieces):
        load(piece).wait()
    for piece in range(pieces):
        pair(half, piece, held.at[me, piece]).wait_recv()

    def compute(arrival, piece):
        feature = origin(arrival, piece)
        slot = feature % half

        @pl.when(feature // half == tok)
        def _():
            @pl.when(arrival > 0)
            def _():
                pair(slot, piece, held.at[feature, piece]).wait_recv()

            own = 1 - (arrival + n - 1) // n
            from_other = own * half + (1 - own) * slot
            multiply(held, other, feature, piece, from_other, tokens, product.at[slot, piece])

    @pl.loop(1, last)
    def _(arrival):
        @pl.loop(0, pieces)
        def _(piece):
            feature = origin(arrival, piece)
            mine = feature // half == tok
            ring(arrival, piece, feature).wait_recv()

            @pl.when((arrival < last - 1) | mine)
            def _():
                ring(arrival + 1, piece, feature).start()

            @pl.when((arrival == last - 1) & (feature // half != tok))
            def _():
                across(piece, feature).start()

            @pl.when(feature // half != tok)
            def _():
                pair(feature % half, piece, held.at[feature, piece]).start()

            compute(arrival - 1, piece)

    @pl.loop(0, pieces)
    def _(piece):
        compute(last - 1, piece)

    @pl.loop(0, pieces)
    def _(piece):
        feature = origin(last, piece)
        slot = feature % half

        @pl.when(feature // half == tok)
        def _():
            ring(last, piece, feature).wait_recv()
            pair(slot, piece, held.at[feature, piece]).wait_recv()

            @pl.when(piece < pieces // 2)
            def _():
                multiply(held, other, feature, piece, slot, tokens, product.at[slot, piece])

    @pl.loop(0, pieces)
    def _(piece):
        @pl.loop(1, last)
        def _(arrival):
            feature = origin(arrival, piece)
            ring(arrival, piece, feature).wait_send()

            @pl.when(feature // half != tok)
            def _():
                pair(feature % half, piece, held.at[feature, piece]).wait_send()

        pair(half, piece, held.at[me, piece]).wait_send()

    @pl.loop(0, pieces)
    def _(piece):
        ring(last, piece, origin(last, piece)).wait_send()


def finish(n, snake, tokens, product, held, other, out_ref, late, sem):
    half, pieces, width, _ = product.shape
    tok, _, origin = position(n, snake)

    def store(slot, piece, src):
        rows = pl.ds(pl.multiple_of((slot * pieces + piece) * width, width), width)
        return pltpu.make_async_copy(src, out_ref.at[rows, :], sem.at[slot, piece])

    @pl.loop(0, half)
    def _(slot):
        @pl.loop(0, pieces)
        def _(piece):
            @pl.when((piece < pieces // 2) | (origin(n - 1, piece) != tok * half + slot))
            def _():
                store(slot, piece, product.at[slot, piece]).start()

    @pl.loop(pieces // 2, pieces)
    def _(piece):
        feature = origin(n - 1, piece)
        slot = feature % half

        @pl.when(feature // half == tok)
        def _():
            multiply(held, other, feature, piece, slot, tokens, late.at[piece])
            store(slot, piece, late.at[piece]).start()

    @pl.loop(0, half)
    def _(slot):
        @pl.loop(0, pieces)
        def _(piece):
            store(slot, piece, product.at[slot, piece]).wait()


def solution(mesh):
    n = mesh.shape["feat"]
    snake = mesh.shape["grp"] == 2

    def shards(states):
        rows, block = states.shape
        tokens = rows * mesh.shape["tok"]
        pieces = max(2, min(4, block // 128))
        width = block // pieces
        half = n // 2
        gathered = pl.pallas_call(
            functools.partial(gather_and_multiply, n, snake, tokens),
            out_shape=(
                pltpu.VMEM((half, pieces, width, block), jnp.float32),
                pltpu.VMEM((n, pieces, rows, width), states.dtype),
                pltpu.VMEM((half + 1, pieces, rows, width), states.dtype),
            ),
            in_specs=[pl.BlockSpec(memory_space=pl.ANY)],
            out_specs=(pl.BlockSpec(memory_space=pltpu.VMEM),) * 3,
            scratch_shapes=[
                pltpu.SemaphoreType.DMA((n - 1, pieces)),
                pltpu.SemaphoreType.DMA((n - 1, pieces)),
                pltpu.SemaphoreType.DMA((half + 1, pieces)),
                pltpu.SemaphoreType.DMA((half + 1, pieces)),
                pltpu.SemaphoreType.DMA((pieces,)),
            ],
            compiler_params=pltpu.CompilerParams(
                collective_id=0, has_side_effects=True, vmem_limit_bytes=10 * 2**20
            ),
            cost_estimate=pl.CostEstimate(
                flops=2 * half * block * block * tokens,
                bytes_accessed=half * block * block * 4 + rows * block * 2,
                transcendentals=0,
            ),
        )(states)
        return pl.pallas_call(
            functools.partial(finish, n, snake, tokens),
            out_shape=jax.ShapeDtypeStruct((half * block, block), jnp.float32),
            in_specs=[pl.BlockSpec(memory_space=pltpu.VMEM)] * 3,
            out_specs=pl.BlockSpec(memory_space=pl.ANY),
            scratch_shapes=[
                pltpu.VMEM((pieces, width, block), jnp.float32),
                pltpu.SemaphoreType.DMA((half, pieces)),
            ],
            compiler_params=pltpu.CompilerParams(vmem_limit_bytes=10 * 2**20),
        )(*(pltpu.with_memory_space_constraint(part, pltpu.VMEM) for part in gathered))

    placed = P(("grp", "tok"), "feat")
    return jax.shard_map(
        shards, mesh=mesh, in_specs=(placed,), out_specs=placed, check_vma=False
    )
```
